32 devices in a mesh: inp: 2 (over y), hid: 4 (over x, core), tok: 4 (over z).
Axes of the slice: x: 2, y: 2, z: 4, core: 2. Of those that a mesh axis runs over, the one named last changes fastest.
Arguments:
- tokens: float32 [512, 3072], P(('tok', 'hid'), 'inp'), may hold values from -6 to 6
- targets: float32 [512, 3072], P(('tok', 'hid'), 'inp'), may hold values from -6 to 6
- sample_ids: int32 [512], P(('tok', 'hid')), may hold values from 0 to 15, never falling along the last dimension, each value on 1 to 64 neighbouring positions
- labels: int32 [16], replicated, may hold values from 0 to 1
- utility: float32 [16], replicated, may hold values from 0.5 to 4
- ref_loss: float32 [16], replicated, may hold values from 0.9 to 1.9
- w_in: float32 [3072, 6144], P(('inp', 'tok'), 'hid'), may hold values from -0.109375 to 0.109375
- w_out: float32 [6144, 3072], P(('hid', 'tok'), 'inp'), may hold values from -0.078125 to 0.078125
- m_in: float32 [3072, 6144], P(('inp', 'tok'), 'hid'), may hold values from -6 to 6
- m_out: float32 [6144, 3072], P(('hid', 'tok'), 'inp'), may hold values from -6 to 6
- v_in: float32 [3072, 6144], P(('inp', 'tok'), 'hid'), may hold values from 0.5 to 20
- v_out: float32 [6144, 3072], P(('hid', 'tok'), 'inp'), may hold values from 0.5 to 20
- e_in: float32 [3072, 6144], P(('inp', 'tok'), 'hid'), may hold values from -0.109375 to 0.109375
- e_out: float32 [6144, 3072], P(('hid', 'tok'), 'inp'), may hold values from -0.078125 to 0.078125
Outputs:
- loss: float32 [], replicated
- new_w_in: float32 [3072, 6144], P('inp', 'hid')
- new_w_out: float32 [6144, 3072], P('hid', 'inp')
- new_m_in: float32 [3072, 6144], P(('inp', 'tok'), 'hid')
- new_m_out: float32 [6144, 3072], P(('hid', 'tok'), 'inp')
- new_v_in: float32 [3072, 6144], P(('inp', 'tok'), 'hid')
- new_v_out: float32 [6144, 3072], P(('hid', 'tok'), 'inp')
- new_e_in: float32 [3072, 6144], P(('inp', 'tok'), 'hid')
- new_e_out: float32 [6144, 3072], P(('hid', 'tok'), 'inp')
The draws below stay inside these ranges and needn't reach their ends.
Inputs may be any that keep to these rules, and one draw needn't show every extreme that they name: `sample_ids`: sample numbers never fall along the tokens; every sample has 1 to 64 tokens, one exactly that many.
All inputs are finite; a program needn't handle non-finite values.
Results may differ from the reference program's by a relative error of at most 0.00022.
Values sent between devices are 32-bit elements; how exact they have to be, the bound alone decides.
A program may use at most 128 MiB of HBM per device.

```python
import math
import jax
import jax.numpy as jnp
import numpy as np
from jax import lax

D = 3072
FF = 6144
SAMPLES = 16
TOKENS = 512


def place_ends(values, key, low, high):
    index_at = [jax.random.randint(jax.random.fold_in(key, axis), (), 0, length) for axis, length in enumerate(values.shape)]
    widest = values.shape.index(max(values.shape))
    next_to = index_at[:widest] + [(index_at[widest] + 1) % values.shape[widest]] + index_at[widest + 1:]
    return values.at[tuple(index_at)].set(low).at[tuple(next_to)].set(high)


def block_levels(own_key, shape, cuts, least, top_value):
    loudness = 1.0
    for dim, shards_of in cuts:
        heights = jax.random.uniform(jax.random.fold_in(jax.random.fold_in(own_key, 6), dim), (shards_of,), jnp.float32, least / len(cuts), top_value / len(cuts))
        loudness = loudness * jnp.repeat(jnp.exp(heights), shape[dim] // shards_of).reshape((-1,) + (1,) * (len(shape) - 1 - dim))
    return loudness


def length_profile(number_of, total, reach, skew):
    portions = [(1 << 20) // math.isqrt(rank ** skew) + 1 for rank in range(2, number_of + 1)]
    rest, given = total - reach - (number_of - 1), [1] * (number_of - 1)
    while rest > 0:
        free = [i for i in range(number_of - 1) if given[i] < reach]
        whole, budget = sum([portions[i] for i in free]), rest
        for i in free:
            addition = min(reach - given[i], max(1, budget * portions[i] // whole), rest)
            given[i] = given[i] + addition
            rest = rest - addition
    return np.array([reach] + given)


def ragged(stream_key, amount, total, limit, lean):
    if amount == 2:
        one = jax.random.randint(stream_key, (), max(1, total - limit), min(limit, total - 1) + 1)
        return jnp.stack([one, total - one])
    tallies = jnp.asarray(length_profile(amount, total, limit, lean), jnp.int32)
    pairs = (amount - 1) // 2
    giver, sink = tallies[1:1 + 2 * pairs:2], tallies[2:2 + 2 * pairs:2]
    margin = jnp.minimum(giver - 1, limit - sink)
    passed = jax.random.randint(jax.random.fold_in(stream_key, 1), (pairs,), 0, 1 << 20) % (margin + 1)
    tallies = tallies.at[1:1 + 2 * pairs:2].set(giver - passed).at[2:2 + 2 * pairs:2].set(sink + passed)
    return tallies[jax.random.permutation(jax.random.fold_in(stream_key, 2), amount)]


def noise(own_key, shape, width, limit, shards=(), held_as=jnp.bfloat16):
    values = jax.random.normal(own_key, shape, jnp.float32) * width
    if len(shards) > 0:
        values = block_levels(own_key, shape, shards, -0.22, 0.18) * values
    return jnp.clip(values, min=-limit, max=limit).astype(held_as)


def setup_inputs(seed: int = 0) -> dict:
    splits = jax.random.split(jax.random.key(seed), 15)
    tokens = noise(splits[0], (TOKENS, D), 1.0, 6.0, ((0, 16), (1, 2)), jnp.float32)
    targets = noise(splits[1], (TOKENS, D), 1.0, 6.0, ((0, 16), (1, 2)), jnp.float32)
    sample_ids = jnp.searchsorted(jnp.cumsum(ragged(splits[2], SAMPLES, TOKENS, 2 * TOKENS // SAMPLES, 0)), jnp.arange(TOKENS), side="right").astype(jnp.int32)
    labels = place_ends(jax.random.randint(splits[3], (SAMPLES,), 0, 2), jax.random.fold_in(splits[3], 1), 0, 1).astype(jnp.int32)
    utility = jnp.clip(jnp.exp(jax.random.uniform(splits[4], (SAMPLES,), jnp.float32, math.log(0.5), math.log(4.0))), 0.5, 4.0)
    ref_loss = jnp.clip(jax.random.uniform(splits[5], (SAMPLES,), jnp.float32, 0.9, 1.9), 0.9, 1.9)
    w_in = noise(splits[6], (D, FF), D ** -0.5, 0.109375, ((0, 8), (1, 4)), jnp.float32)
    w_out = noise(splits[7], (FF, D), FF ** -0.5, 0.078125, ((0, 16), (1, 2)), jnp.float32)
    m_in = noise(splits[8], (D, FF), 1.0, 6.0, ((0, 8), (1, 4)), jnp.float32)
    m_out = noise(splits[9], (FF, D), 1.0, 6.0, ((0, 16), (1, 2)), jnp.float32)
    v_in = jnp.clip(jnp.exp(math.log(20.0) - 3.6888795 * jax.random.uniform(splits[10], (D, FF), jnp.float32) ** block_levels(splits[10], (D, FF), ((0, 8), (1, 4)), -0.2, 0.2)), 0.5, 20.0)
    v_out = jnp.clip(jnp.exp(math.log(20.0) - 3.6888795 * jax.random.uniform(splits[11], (FF, D), jnp.float32) ** block_levels(splits[11], (FF, D), ((0, 16), (1, 2)), -0.2, 0.2)), 0.5, 20.0)
    e_in = noise(splits[12], (D, FF), D ** -0.5, 0.109375, ((0, 8), (1, 4)), jnp.float32)
    e_out = noise(splits[13], (FF, D), FF ** -0.5, 0.078125, ((0, 16), (1, 2)), jnp.float32)
    return {"tokens": tokens, "targets": targets, "sample_ids": sample_ids, "labels": labels, "utility": utility, "ref_loss": ref_loss, "w_in": w_in, "w_out": w_out, "m_in": m_in, "m_out": m_out, "v_in": v_in, "v_out": v_out, "e_in": e_in, "e_out": e_out}


highest = lax.Precision.HIGHEST
gelu_c = 0.7978845608028654
gelu_k = 0.044715
kto_beta = 4.0
loss_scale = 1048576.0
beta_one = 0.9
beta_two = 0.95
adam_eps = 1e-08
learn_rate = 0.001
decay_rate = 0.1
ema_rate = 0.99
bias_one = 1.0 - 0.9 ** 10
bias_two = 1.0 - 0.95 ** 10

def gelu_parts(hidden):
    inner = gelu_c * (hidden + gelu_k * hidden * hidden * hidden)
    tangent = jnp.tanh(inner)
    active = 0.5 * hidden * (1.0 + tangent)
    slope = 0.5 * (1.0 + tangent) + 0.5 * hidden * (1.0 - tangent * tangent) * gelu_c * (1.0 + 3.0 * gelu_k * hidden * hidden)
    return (active, slope)

def adamw(weight, moment_one, moment_two, average, gradient):
    moment_one = beta_one * moment_one + (1.0 - beta_one) * gradient
    moment_two = beta_two * moment_two + (1.0 - beta_two) * gradient * gradient
    update = learn_rate * (moment_one / bias_one) / (jnp.sqrt(moment_two / bias_two) + adam_eps)
    weight = weight - update - learn_rate * decay_rate * weight
    average = ema_rate * average + (1.0 - ema_rate) * weight
    return (weight, moment_one, moment_two, average)

def kto_terms(sq_sums, counts, labels, utility, ref_loss):
    sample_loss = sq_sums / (counts * D)
    signs = 2.0 * labels.astype(jnp.float32) - 1.0
    chosen = jax.nn.sigmoid(signs * kto_beta * (ref_loss - sample_loss))
    loss = -jnp.sum(utility * chosen) / SAMPLES
    dloss = utility * chosen * (1.0 - chosen) * signs * kto_beta / SAMPLES
    sample_coef = loss_scale * 2.0 * dloss / (counts * D)
    return (loss, sample_coef)

def reference(tokens, targets, sample_ids, labels, utility, ref_loss, w_in, w_out, m_in, m_out, v_in, v_out, e_in, e_out):
    hidden = jnp.dot(tokens, w_in, precision=highest, preferred_element_type=jnp.float32)
    active, slope = gelu_parts(hidden)
    output = jnp.dot(active, w_out, precision=highest, preferred_element_type=jnp.float32)
    error_rows = output - targets
    onehot = (sample_ids[:, None] == jnp.arange(SAMPLES, dtype=jnp.int32)[None, :]).astype(jnp.float32)
    token_sq = lax.optimization_barrier(jnp.sum(error_rows * error_rows, axis=1))
    sq_sums = jnp.dot(token_sq, onehot, precision=highest)
    counts = lax.optimization_barrier(jnp.sum(onehot, axis=0))
    loss, sample_coef = kto_terms(sq_sums, counts, labels, utility, ref_loss)
    d_output = error_rows * jnp.dot(onehot, sample_coef, precision=highest)[:, None]
    grad_out = lax.dot_general(active, d_output, (((0,), (0,)), ((), ())), precision=highest)
    d_active = lax.dot_general(d_output, w_out, (((1,), (1,)), ((), ())), precision=highest)
    d_hidden = d_active * slope
    grad_in = lax.dot_general(tokens, d_hidden, (((0,), (0,)), ((), ())), precision=highest)
    new_w_in, new_m_in, new_v_in, new_e_in = adamw(w_in, m_in, v_in, e_in, grad_in)
    new_w_out, new_m_out, new_v_out, new_e_out = adamw(w_out, m_out, v_out, e_out, grad_out)
    return (loss, new_w_in, new_w_out, new_m_in, new_m_out, new_v_in, new_v_out, new_e_in, new_e_out)
```

```python
import jax
import jax.numpy as jnp
from jax import lax
from jax.sharding import PartitionSpec as P

D = 3072
SAMPLES = 16


highest = lax.Precision.HIGHEST
precise = lax.Precision.HIGH
gelu_c = 0.7978845608028654
gelu_k = 0.044715
kto_beta = 4.0
loss_scale = 1048576.0
beta_one = 0.9
beta_two = 0.95
adam_eps = 1e-08
learn_rate = 0.001
decay_rate = 0.1
ema_rate = 0.99
bias_one = 1.0 - 0.9**10
bias_two = 1.0 - 0.95**10


def gelu_parts(hidden):
    inner = gelu_c * (hidden + gelu_k * hidden * hidden * hidden)
    tangent = jnp.tanh(inner)
    active = 0.5 * hidden * (1.0 + tangent)
    slope = 0.5 * (1.0 + tangent) + 0.5 * hidden * (1.0 - tangent * tangent) * gelu_c * (
        1.0 + 3.0 * gelu_k * hidden * hidden
    )
    return (active, slope)


def adamw(weight, moment_one, moment_two, average, gradient):
    moment_one = beta_one * moment_one + (1.0 - beta_one) * gradient
    moment_two = beta_two * moment_two + (1.0 - beta_two) * gradient * gradient
    update = learn_rate * (moment_one / bias_one) / (jnp.sqrt(moment_two / bias_two) + adam_eps)
    weight = weight - update - learn_rate * decay_rate * weight
    average = ema_rate * average + (1.0 - ema_rate) * weight
    return (weight, moment_one, moment_two, average)


def kto_terms(sq_sums, counts, labels, utility, ref_loss):
    sample_loss = sq_sums / (counts * D)
    signs = 2.0 * labels.astype(jnp.float32) - 1.0
    chosen = jax.nn.sigmoid(signs * kto_beta * (ref_loss - sample_loss))
    loss = -jnp.sum(utility * chosen) / SAMPLES
    dloss = utility * chosen * (1.0 - chosen) * signs * kto_beta / SAMPLES
    sample_coef = loss_scale * 2.0 * dloss / (counts * D)
    return (loss, sample_coef)


def contract_rows(left, right):
    return lax.dot_general(left, right, (((0,), (0,)), ((), ())), precision=precise)


def gather_rows(block, axis):
    return lax.all_gather(block, axis, axis=0, tiled=True)


def scatter_rows(part, axis):
    return lax.psum_scatter(part, axis, scatter_dimension=0, tiled=True)


def on_device(
    tokens,
    targets,
    sample_ids,
    labels,
    utility,
    ref_loss,
    w_in,
    w_out,
    m_in,
    m_out,
    v_in,
    v_out,
    e_in,
    e_out,
):
    ids = gather_rows(gather_rows(sample_ids, "tok"), "hid")
    onehot = (ids[:, None] == jnp.arange(SAMPLES, dtype=jnp.int32)[None, :]).astype(jnp.float32)
    counts = jnp.sum(onehot, axis=0)
    columns = lax.all_to_all(tokens, "tok", split_axis=1, concat_axis=0, tiled=True)
    all_rows = gather_rows(columns, "hid")
    hidden_part = lax.dot_general(w_in, all_rows, (((0,), (1,)), ((), ())), precision=precise)
    hidden = lax.psum(scatter_rows(hidden_part, "tok"), "inp")
    active, slope = gelu_parts(hidden)
    out_part = contract_rows(active, w_out)
    output = scatter_rows(scatter_rows(out_part, "hid"), "tok")
    error = gather_rows(gather_rows(output - targets, "tok"), "hid")
    token_sq = jnp.sum(error * error, axis=1)
    sq_sums = lax.psum(jnp.dot(token_sq, onehot, precision=highest), "inp")
    loss, sample_coef = kto_terms(sq_sums, counts, labels, utility, ref_loss)
    token_coef = jnp.dot(onehot, sample_coef, precision=highest)
    grad_out = jnp.dot(active * token_coef[None, :], error, precision=precise)
    d_active = lax.psum(
        lax.dot_general(w_out, error, (((1,), (1,)), ((), ())), precision=precise), "inp"
    )
    d_hidden = gather_rows(d_active * slope * token_coef[None, :], "tok")
    weight_out, new_m_out, new_v_out, new_e_out = adamw(w_out, m_out, v_out, e_out, grad_out)
    new_w_out = gather_rows(weight_out, "tok")
    grad_in = lax.dot_general(all_rows, d_hidden, (((0,), (1,)), ((), ())), precision=precise)
    weight_in, new_m_in, new_v_in, new_e_in = adamw(w_in, m_in, v_in, e_in, grad_in)
    new_w_in = gather_rows(weight_in, "tok")
    return (
        loss,
        new_w_in,
        new_w_out,
        new_m_in,
        new_m_out,
        new_v_in,
        new_v_out,
        new_e_in,
        new_e_out,
    )


def solution(mesh):
    in_specs = (
        P(("tok", "hid"), "inp"),
        P(("tok", "hid"), "inp"),
        P(("tok", "hid")),
        P(),
        P(),
        P(),
        P(("inp", "tok"), "hid"),
        P(("hid", "tok"), "inp"),
        P(("inp", "tok"), "hid"),
        P(("hid", "tok"), "inp"),
        P(("inp", "tok"), "hid"),
        P(("hid", "tok"), "inp"),
        P(("inp", "tok"), "hid"),
        P(("hid", "tok"), "inp"),
    )
    out_specs = (
        P(),
        P("inp", "hid"),
        P("hid", "inp"),
        P(("inp", "tok"), "hid"),
        P(("hid", "tok"), "inp"),
        P(("inp", "tok"), "hid"),
        P(("hid", "tok"), "inp"),
        P(("inp", "tok"), "hid"),
        P(("hid", "tok"), "inp"),
    )
    return jax.shard_map(
        on_device, mesh=mesh, in_specs=in_specs, out_specs=out_specs, check_vma=False
    )
```

```python
import jax
import jax.numpy as jnp
from jax import lax
from jax.sharding import PartitionSpec as P

D = 3072
SAMPLES = 16


highest = lax.Precision.HIGHEST
precise = lax.Precision.HIGH
gelu_c = 0.7978845608028654
gelu_k = 0.044715
kto_beta = 4.0
loss_scale = 1048576.0
beta_one = 0.9
beta_two = 0.95
adam_eps = 1e-08
learn_rate = 0.001
decay_rate = 0.1
ema_rate = 0.99
bias_one = 1.0 - 0.9**10
bias_two = 1.0 - 0.95**10


def gelu_parts(hidden):
    inner = gelu_c * (hidden + gelu_k * hidden * hidden * hidden)
    tangent = jnp.tanh(inner)
    active = 0.5 * hidden * (1.0 + tangent)
    slope = 0.5 * (1.0 + tangent) + 0.5 * hidden * (1.0 - tangent * tangent) * gelu_c * (
        1.0 + 3.0 * gelu_k * hidden * hidden
    )
    return (active, slope)


def adamw(weight, moment_one, moment_two, average, gradient):
    moment_one = beta_one * moment_one + (1.0 - beta_one) * gradient
    moment_two = beta_two * moment_two + (1.0 - beta_two) * gradient * gradient
    update = learn_rate * (moment_one / bias_one) / (jnp.sqrt(moment_two / bias_two) + adam_eps)
    weight = weight - update - learn_rate * decay_rate * weight
    average = ema_rate * average + (1.0 - ema_rate) * weight
    return (weight, moment_one, moment_two, average)


def kto_terms(sq_sums, counts, labels, utility, ref_loss):
    sample_loss = sq_sums / (counts * D)
    signs = 2.0 * labels.astype(jnp.float32) - 1.0
    chosen = jax.nn.sigmoid(signs * kto_beta * (ref_loss - sample_loss))
    loss = -jnp.sum(utility * chosen) / SAMPLES
    dloss = utility * chosen * (1.0 - chosen) * signs * kto_beta / SAMPLES
    sample_coef = loss_scale * 2.0 * dloss / (counts * D)
    return (loss, sample_coef)


def contract_rows(left, right):
    return lax.dot_general(left, right, (((0,), (0,)), ((), ())), precision=precise)


def gather_rows(block, axis):
    return lax.all_gather(block, axis, axis=0, tiled=True)


def scatter_rows(part, axis):
    return lax.psum_scatter(part, axis, scatter_dimension=0, tiled=True)


def spread_rows(block, axis):
    size = lax.axis_size(axis)
    before, after = [], []
    rightward = leftward = block
    for step in range(size - 1):
        rightward = lax.ppermute(rightward, axis, [(i, i + 1) for i in range(step, size - 1)])
        leftward = lax.ppermute(leftward, axis, [(i + 1, i) for i in range(size - 1 - step)])
        before.insert(0, rightward)
        after.append(leftward)
    line = jnp.concatenate(before + [block] + after, axis=0)
    rows = block.shape[0]
    start = (size - 1 - lax.axis_index(axis)) * rows
    return lax.dynamic_slice_in_dim(line, start, size * rows, axis=0)


def on_device(
    tokens,
    targets,
    sample_ids,
    labels,
    utility,
    ref_loss,
    w_in,
    w_out,
    m_in,
    m_out,
    v_in,
    v_out,
    e_in,
    e_out,
):
    ids = gather_rows(gather_rows(sample_ids, "tok"), "hid")
    onehot = (ids[:, None] == jnp.arange(SAMPLES, dtype=jnp.int32)[None, :]).astype(jnp.float32)
    counts = jnp.sum(onehot, axis=0)
    columns = lax.all_to_all(tokens, "tok", split_axis=1, concat_axis=0, tiled=True)
    all_rows = gather_rows(columns, "hid")
    hidden_part = lax.dot_general(w_in, all_rows, (((0,), (1,)), ((), ())), precision=precise)
    hidden = lax.psum(scatter_rows(hidden_part, "tok"), "inp")
    active, slope = gelu_parts(hidden)
    out_part = contract_rows(active, w_out)
    output = scatter_rows(scatter_rows(out_part, "hid"), "tok")
    error = gather_rows(gather_rows(output - targets, "tok"), "hid")
    token_sq = jnp.sum(error * error, axis=1)
    sq_sums = lax.psum(jnp.dot(token_sq, onehot, precision=highest), "inp")
    loss, sample_coef = kto_terms(sq_sums, counts, labels, utility, ref_loss)
    token_coef = jnp.dot(onehot, sample_coef, precision=highest)
    grad_out = jnp.dot(active * token_coef[None, :], error, precision=precise)
    d_active = lax.psum(
        lax.dot_general(w_out, error, (((1,), (1,)), ((), ())), precision=precise), "inp"
    )
    d_hidden = gather_rows(d_active * slope * token_coef[None, :], "tok")
    weight_out, new_m_out, new_v_out, new_e_out = adamw(w_out, m_out, v_out, e_out, grad_out)
    new_w_out = spread_rows(weight_out, "tok")
    grad_in = lax.dot_general(all_rows, d_hidden, (((0,), (1,)), ((), ())), precision=precise)
    weight_in, new_m_in, new_v_in, new_e_in = adamw(w_in, m_in, v_in, e_in, grad_in)
    new_w_in = spread_rows(weight_in, "tok")
    return (
        loss,
        new_w_in,
        new_w_out,
        new_m_in,
        new_m_out,
        new_v_in,
        new_v_out,
        new_e_in,
        new_e_out,
    )


def solution(mesh):
    in_specs = (
        P(("tok", "hid"), "inp"),
        P(("tok", "hid"), "inp"),
        P(("tok", "hid")),
        P(),
        P(),
        P(),
        P(("inp", "tok"), "hid"),
        P(("hid", "tok"), "inp"),
        P(("inp", "tok"), "hid"),
        P(("hid", "tok"), "inp"),
        P(("inp", "tok"), "hid"),
        P(("hid", "tok"), "inp"),
        P(("inp", "tok"), "hid"),
        P(("hid", "tok"), "inp"),
    )
    out_specs = (
        P(),
        P("inp", "hid"),
        P("hid", "inp"),
        P(("inp", "tok"), "hid"),
        P(("hid", "tok"), "inp"),
        P(("inp", "tok"), "hid"),
        P(("hid", "tok"), "inp"),
        P(("inp", "tok"), "hid"),
        P(("hid", "tok"), "inp"),
    )
    return jax.shard_map(
        on_device, mesh=mesh, in_specs=in_specs, out_specs=out_specs, check_vma=False
    )
```

```python
import functools

import jax
import jax.numpy as jnp
from jax import lax
from jax.experimental import pallas as pl
from jax.experimental.pallas import tpu as pltpu
from jax.sharding import PartitionSpec as P

D = 3072
SAMPLES = 16


highest = lax.Precision.HIGHEST
precise = lax.Precision.HIGH
gelu_c = 0.7978845608028654
gelu_k = 0.044715
kto_beta = 4.0
loss_scale = 1048576.0
beta_one = 0.9
beta_two = 0.95
adam_eps = 1e-08
learn_rate = 0.001
decay_rate = 0.1
ema_rate = 0.99
bias_one = 1.0 - 0.9**10
bias_two = 1.0 - 0.95**10


def gelu_parts(hidden):
    inner = gelu_c * (hidden + gelu_k * hidden * hidden * hidden)
    tangent = jnp.tanh(inner)
    active = 0.5 * hidden * (1.0 + tangent)
    slope = 0.5 * (1.0 + tangent) + 0.5 * hidden * (1.0 - tangent * tangent) * gelu_c * (
        1.0 + 3.0 * gelu_k * hidden * hidden
    )
    return (active, slope)


def adamw(weight, moment_one, moment_two, average, gradient):
    moment_one = beta_one * moment_one + (1.0 - beta_one) * gradient
    moment_two = beta_two * moment_two + (1.0 - beta_two) * gradient * gradient
    update = learn_rate * (moment_one / bias_one) / (jnp.sqrt(moment_two / bias_two) + adam_eps)
    weight = weight - update - learn_rate * decay_rate * weight
    average = ema_rate * average + (1.0 - ema_rate) * weight
    return (weight, moment_one, moment_two, average)


def kto_terms(sq_sums, counts, labels, utility, ref_loss):
    sample_loss = sq_sums / (counts * D)
    signs = 2.0 * labels.astype(jnp.float32) - 1.0
    chosen = jax.nn.sigmoid(signs * kto_beta * (ref_loss - sample_loss))
    loss = -jnp.sum(utility * chosen) / SAMPLES
    dloss = utility * chosen * (1.0 - chosen) * signs * kto_beta / SAMPLES
    sample_coef = loss_scale * 2.0 * dloss / (counts * D)
    return (loss, sample_coef)


def contract_rows(left, right):
    return lax.dot_general(left, right, (((0,), (0,)), ((), ())), precision=precise)


def gather_rows(block, axis):
    return lax.all_gather(block, axis, axis=0, tiled=True)


def scatter_rows(part, axis):
    return lax.psum_scatter(part, axis, scatter_dimension=0, tiled=True)


def split_bf16(value):
    high = value.astype(jnp.bfloat16)
    return high, (value - high.astype(jnp.float32)).astype(jnp.bfloat16)


def tail_kernel(
    size,
    parts,
    d_part,
    scale,
    rows_t,
    w_in,
    m_in,
    v_in,
    e_in,
    w_out,
    all_in,
    all_out,
    m_new,
    v_new,
    e_new,
    others,
    d_all,
    w_new,
    rows_high,
    rows_low,
    part_send,
    part_recv,
    line_send,
    line_recv,
    own_sem,
):
    me = lax.axis_index("tok")
    part = lax.axis_index("inp")
    units, depth = d_part.shape[0], rows_t.shape[0]
    mesh_ids = pl.DeviceIdType.MESH
    steps = size - 1
    has_left, has_right = me > 0, me < size - 1

    barrier = pltpu.get_barrier_semaphore()
    for hop in range(1, parts):
        peer = lax.rem(part + hop, parts)
        pl.semaphore_signal(barrier, inc=1, device_id={"inp": peer}, device_id_type=mesh_ids)

    @pl.when(has_left)
    def _():
        pl.semaphore_signal(barrier, inc=1, device_id={"tok": me - 1}, device_id_type=mesh_ids)

    @pl.when(has_right)
    def _():
        pl.semaphore_signal(barrier, inc=1, device_id={"tok": me + 1}, device_id_type=mesh_ids)

    beside = has_left.astype(jnp.int32) + has_right.astype(jnp.int32)
    pl.semaphore_wait(barrier, parts - 1 + beside)

    def part_copy(hop):
        return pltpu.make_async_remote_copy(
            src_ref=d_part,
            dst_ref=others.at[hop - 1],
            send_sem=part_send.at[hop - 1],
            recv_sem=part_recv.at[hop - 1],
            device_id={"inp": lax.rem(part + hop, parts)},
            device_id_type=mesh_ids,
        )

    for hop in range(1, parts):
        part_copy(hop).start()

    def line_copy(kind, way, step, shard, own=None):
        array, rows = ((d_all, units), (all_out, units), (all_in, depth))[kind]
        place = array.at[pl.ds(shard * rows, rows)]
        return pltpu.make_async_remote_copy(
            src_ref=place if own is None else own,
            dst_ref=place,
            send_sem=line_send.at[kind, way, step],
            recv_sem=line_recv.at[kind, way, step],
            device_id={"tok": me + (1 if way == 0 else -1)},
            device_id_type=mesh_ids,
        )

    def send_own(kind, own):
        @pl.when(has_right)
        def _():
            line_copy(kind, 0, 0, me, own).start()

        @pl.when(has_left)
        def _():
            line_copy(kind, 1, 0, me, own).start()

    def pass_on(kind, step):
        @pl.when(me - 1 - step >= 0)
        def _():
            line_copy(kind, 0, step, me - 1 - step).wait_recv()
            if step + 1 < steps:

                @pl.when(has_right)
                def _():
                    line_copy(kind, 0, step + 1, me - 1 - step).start()

        @pl.when(me + 1 + step < size)
        def _():
            line_copy(kind, 1, step, me + 1 + step).wait_recv()
            if step + 1 < steps:

                @pl.when(has_left)
                def _():
                    line_copy(kind, 1, step + 1, me + 1 + step).start()

    def end_sends(kind):
        for step in range(steps):

            @pl.when((me - step >= 0) & has_right)
            def _():
                line_copy(kind, 0, step, me - step).wait_send()

            @pl.when((me + step < size) & has_left)
            def _():
                line_copy(kind, 1, step, me + step).wait_send()

    own_out = pltpu.make_async_copy(w_out, all_out.at[pl.ds(me * units, units)], own_sem.at[0])
    send_own(1, w_out)
    own_out.start()
    high, low = split_bf16(rows_t[...])
    rows_high[...] = high
    rows_low[...] = low

    for hop in range(1, parts):
        part_copy(hop).wait_recv()
    mine = pl.ds(me * units, units)
    total = d_part[...]
    for hop in range(1, parts):
        total = total + others[hop - 1]
    d_all[mine, :] = total * scale[...]
    send_own(0, d_all.at[mine])

    early = max(steps - 1, 0)
    for step in range(early):
        pass_on(0, step)
    pass_on(1, 0)
    for step in range(early, steps):
        pass_on(0, step)

    width = 256

    @pl.loop(0, w_in.shape[1] // width)
    def _(tile):
        cols = pl.ds(pl.multiple_of(tile * width, width), width)
        d_high, d_low = split_bf16(d_all[cols, :])

        def product(left, right):
            return lax.dot_general(
                left, right, (((1,), (1,)), ((), ())), preferred_element_type=jnp.float32
            )

        grad = product(rows_high[...], d_high)
        grad = grad + (product(rows_low[...], d_high) + product(rows_high[...], d_low))
        weight, moment_one, moment_two, average = adamw(
            w_in[:, cols], m_in[:, cols], v_in[:, cols], e_in[:, cols], grad
        )
        w_new[:, cols] = weight
        m_new[:, cols] = moment_one
        v_new[:, cols] = moment_two
        e_new[:, cols] = average

    own_in = pltpu.make_async_copy(w_new, all_in.at[pl.ds(me * depth, depth)], own_sem.at[1])
    send_own(2, w_new)
    own_in.start()
    for step in range(steps):
        if step + 1 < steps:
            pass_on(1, step + 1)
        pass_on(2, step)
    for hop in range(1, parts):
        part_copy(hop).wait_send()
    for kind in range(3):
        end_sends(kind)
    own_out.wait()
    own_in.wait()


def backward_tail(d_part, scale, rows_t, w_in, m_in, v_in, e_in, w_out):
    size, parts = lax.axis_size("tok"), lax.axis_size("inp")
    units, count = d_part.shape
    depth, wide = w_in.shape
    hops, steps = max(parts - 1, 1), max(size - 1, 1)
    in_vmem = pl.BlockSpec(memory_space=pltpu.VMEM)
    anywhere = pl.BlockSpec(memory_space=pl.ANY)
    shard = jax.ShapeDtypeStruct((depth, wide), jnp.float32)
    return pl.pallas_call(
        functools.partial(tail_kernel, size, parts),
        out_shape=(
            jax.ShapeDtypeStruct((size * depth, wide), jnp.float32),
            jax.ShapeDtypeStruct((size * units, w_out.shape[1]), jnp.float32),
            shard,
            shard,
            shard,
        ),
        in_specs=[in_vmem] * 7 + [anywhere],
        out_specs=(anywhere, anywhere, in_vmem, in_vmem, in_vmem),
        scratch_shapes=[
            pltpu.VMEM((hops, units, count), jnp.float32),
            pltpu.VMEM((size * units, count), jnp.float32),
            pltpu.VMEM((depth, wide), jnp.float32),
            pltpu.VMEM((depth, count), jnp.bfloat16),
            pltpu.VMEM((depth, count), jnp.bfloat16),
            pltpu.SemaphoreType.DMA((hops,)),
            pltpu.SemaphoreType.DMA((hops,)),
            pltpu.SemaphoreType.DMA((3, 2, steps)),
            pltpu.SemaphoreType.DMA((3, 2, steps)),
            pltpu.SemaphoreType.DMA((2,)),
        ],
        compiler_params=pltpu.CompilerParams(
            collective_id=0, has_side_effects=True, vmem_limit_bytes=48 * 1024 * 1024
        ),
    )(d_part, scale, rows_t, w_in, m_in, v_in, e_in, w_out)


def on_device(
    tokens,
    targets,
    sample_ids,
    labels,
    utility,
    ref_loss,
    w_in,
    w_out,
    m_in,
    m_out,
    v_in,
    v_out,
    e_in,
    e_out,
):
    ids = gather_rows(gather_rows(sample_ids, "tok"), "hid")
    onehot = (ids[:, None] == jnp.arange(SAMPLES, dtype=jnp.int32)[None, :]).astype(jnp.float32)
    counts = jnp.sum(onehot, axis=0)
    columns = lax.all_to_all(tokens, "tok", split_axis=1, concat_axis=0, tiled=True)
    all_rows = gather_rows(columns, "hid")
    hidden_part = lax.dot_general(w_in, all_rows, (((0,), (1,)), ((), ())), precision=precise)
    hidden = lax.psum(scatter_rows(hidden_part, "tok"), "inp")
    active, slope = gelu_parts(hidden)
    out_part = contract_rows(active, w_out)
    output = scatter_rows(scatter_rows(out_part, "hid"), "tok")
    error = gather_rows(gather_rows(output - targets, "tok"), "hid")
    token_sq = jnp.sum(error * error, axis=1)
    sq_sums = lax.psum(jnp.dot(token_sq, onehot, precision=highest), "inp")
    loss, sample_coef = kto_terms(sq_sums, counts, labels, utility, ref_loss)
    token_coef = jnp.dot(onehot, sample_coef, precision=highest)
    grad_out = jnp.dot(active * token_coef[None, :], error, precision=precise)
    d_part = lax.dot_general(w_out, error, (((1,), (1,)), ((), ())), precision=precise)
    weight_out, new_m_out, new_v_out, new_e_out = adamw(w_out, m_out, v_out, e_out, grad_out)
    new_w_in, new_w_out, new_m_in, new_v_in, new_e_in = backward_tail(
        d_part, slope * token_coef[None, :], all_rows.T, w_in, m_in, v_in, e_in, weight_out
    )
    return (
        loss,
        new_w_in,
        new_w_out,
        new_m_in,
        new_m_out,
        new_v_in,
        new_v_out,
        new_e_in,
        new_e_out,
    )


def solution(mesh):
    in_specs = (
        P(("tok", "hid"), "inp"),
        P(("tok", "hid"), "inp"),
        P(("tok", "hid")),
        P(),
        P(),
        P(),
        P(("inp", "tok"), "hid"),
        P(("hid", "tok"), "inp"),
        P(("inp", "tok"), "hid"),
        P(("hid", "tok"), "inp"),
        P(("inp", "tok"), "hid"),
        P(("hid", "tok"), "inp"),
        P(("inp", "tok"), "hid"),
        P(("hid", "tok"), "inp"),
    )
    out_specs = (
        P(),
        P("inp", "hid"),
        P("hid", "inp"),
        P(("inp", "tok"), "hid"),
        P(("hid", "tok"), "inp"),
        P(("inp", "tok"), "hid"),
        P(("hid", "tok"), "inp"),
        P(("inp", "tok"), "hid"),
        P(("hid", "tok"), "inp"),
    )
    return jax.shard_map(
        on_device, mesh=mesh, in_specs=in_specs, out_specs=out_specs, check_vma=False
    )
```

```python
import functools

import jax
import jax.numpy as jnp
from jax import lax
from jax.experimental import pallas as pl
from jax.experimental.pallas import tpu as pltpu
from jax.sharding import PartitionSpec as P

D = 3072
SAMPLES = 16


highest = lax.Precision.HIGHEST
precise = lax.Precision.HIGH
gelu_c = 0.7978845608028654
gelu_k = 0.044715
kto_beta = 4.0
loss_scale = 1048576.0
beta_one = 0.9
beta_two = 0.95
adam_eps = 1e-08
learn_rate = 0.001
decay_rate = 0.1
ema_rate = 0.99
bias_one = 1.0 - 0.9**10
bias_two = 1.0 - 0.95**10


def gelu_parts(hidden):
    inner = gelu_c * (hidden + gelu_k * hidden * hidden * hidden)
    tangent = jnp.tanh(inner)
    active = 0.5 * hidden * (1.0 + tangent)
    slope = 0.5 * (1.0 + tangent) + 0.5 * hidden * (1.0 - tangent * tangent) * gelu_c * (
        1.0 + 3.0 * gelu_k * hidden * hidden
    )
    return (active, slope)


def adamw(weight, moment_one, moment_two, average, gradient):
    moment_one = beta_one * moment_one + (1.0 - beta_one) * gradient
    moment_two = beta_two * moment_two + (1.0 - beta_two) * gradient * gradient
    update = learn_rate * (moment_one / bias_one) / (jnp.sqrt(moment_two / bias_two) + adam_eps)
    weight = weight - update - learn_rate * decay_rate * weight
    average = ema_rate * average + (1.0 - ema_rate) * weight
    return (weight, moment_one, moment_two, average)


def kto_terms(sq_sums, counts, labels, utility, ref_loss):
    sample_loss = sq_sums / (counts * D)
    signs = 2.0 * labels.astype(jnp.float32) - 1.0
    chosen = jax.nn.sigmoid(signs * kto_beta * (ref_loss - sample_loss))
    loss = -jnp.sum(utility * chosen) / SAMPLES
    dloss = utility * chosen * (1.0 - chosen) * signs * kto_beta / SAMPLES
    sample_coef = loss_scale * 2.0 * dloss / (counts * D)
    return (loss, sample_coef)


def contract_rows(left, right):
    return lax.dot_general(left, right, (((0,), (0,)), ((), ())), precision=precise)


def gather_rows(block, axis):
    return lax.all_gather(block, axis, axis=0, tiled=True)


def scatter_rows(part, axis):
    return lax.psum_scatter(part, axis, scatter_dimension=0, tiled=True)


def split_bf16(value):
    high = value.astype(jnp.bfloat16)
    return high, (value - high.astype(jnp.float32)).astype(jnp.bfloat16)


def tail_kernel(
    size,
    parts,
    d_part,
    scale,
    rows_t,
    w_in,
    m_in,
    v_in,
    e_in,
    w_out,
    all_in,
    all_out,
    m_new,
    v_new,
    e_new,
    others,
    d_all,
    w_new,
    rows_high,
    rows_low,
    part_send,
    part_recv,
    line_send,
    line_recv,
    spread_send,
    spread_recv,
    own_sem,
):
    me = lax.axis_index("tok")
    part = lax.axis_index("inp")
    units, depth = d_part.shape[0], rows_t.shape[0]
    block = d_part.shape[1] // parts

    def block_of(index):
        return pl.ds(pl.multiple_of(index * block, block), block)

    my_block = block_of(part)
    mesh_ids = pl.DeviceIdType.MESH
    steps = size - 1
    has_left, has_right = me > 0, me < size - 1

    barrier = pltpu.get_barrier_semaphore()
    for hop in range(1, parts):
        peer = lax.rem(part + hop, parts)
        pl.semaphore_signal(barrier, inc=1, device_id={"inp": peer}, device_id_type=mesh_ids)

    @pl.when(has_left)
    def _():
        pl.semaphore_signal(barrier, inc=1, device_id={"tok": me - 1}, device_id_type=mesh_ids)

    @pl.when(has_right)
    def _():
        pl.semaphore_signal(barrier, inc=1, device_id={"tok": me + 1}, device_id_type=mesh_ids)

    beside = has_left.astype(jnp.int32) + has_right.astype(jnp.int32)
    pl.semaphore_wait(barrier, parts - 1 + beside)

    def part_copy(hop):
        return pltpu.make_async_remote_copy(
            src_ref=d_part.at[:, block_of(lax.rem(part + hop, parts))],
            dst_ref=others.at[hop - 1],
            send_sem=part_send.at[hop - 1],
            recv_sem=part_recv.at[hop - 1],
            device_id={"inp": lax.rem(part + hop, parts)},
            device_id_type=mesh_ids,
        )

    for hop in range(1, parts):
        part_copy(hop).start()

    def line_copy(kind, way, step, shard, own=None):
        array, rows = ((d_all, units), (all_out, units), (all_in, depth))[kind]
        place = array.at[pl.ds(shard * rows, rows)]
        if kind == 0:
            place = d_all.at[pl.ds(shard * rows, rows), my_block]
        return pltpu.make_async_remote_copy(
            src_ref=place if own is None else own,
            dst_ref=place,
            send_sem=line_send.at[kind, way, step],
            recv_sem=line_recv.at[kind, way, step],
            device_id={"tok": me + (1 if way == 0 else -1)},
            device_id_type=mesh_ids,
        )

    def spread(hop, shard, source):
        place = d_all.at[pl.ds(shard * units, units), block_of(source)]
        return pltpu.make_async_remote_copy(
            src_ref=place,
            dst_ref=place,
            send_sem=spread_send.at[hop - 1, shard],
            recv_sem=spread_recv.at[hop - 1, shard],
            device_id={"inp": lax.rem(part + hop, parts)},
            device_id_type=mesh_ids,
        )

    def start_spread(shard):
        for hop in range(1, parts):
            spread(hop, shard, part).start()

    def send_own(kind, own):
        @pl.when(has_right)
        def _():
            line_copy(kind, 0, 0, me, own).start()

        @pl.when(has_left)
        def _():
            line_copy(kind, 1, 0, me, own).start()

    def pass_on(kind, step):
        @pl.when(me - 1 - step >= 0)
        def _():
            line_copy(kind, 0, step, me - 1 - step).wait_recv()
            if kind == 0:
                start_spread(me - 1 - step)
            if step + 1 < steps:

                @pl.when(has_right)
                def _():
                    line_copy(kind, 0, step + 1, me - 1 - step).start()

        @pl.when(me + 1 + step < size)
        def _():
            line_copy(kind, 1, step, me + 1 + step).wait_recv()
            if kind == 0:
                start_spread(me + 1 + step)
            if step + 1 < steps:

                @pl.when(has_left)
                def _():
                    line_copy(kind, 1, step + 1, me + 1 + step).start()

    def end_sends(kind):
        for step in range(steps):

            @pl.when((me - step >= 0) & has_right)
            def _():
                line_copy(kind, 0, step, me - step).wait_send()

            @pl.when((me + step < size) & has_left)
            def _():
                line_copy(kind, 1, step, me + step).wait_send()

    own_out = pltpu.make_async_copy(w_out, all_out.at[pl.ds(me * units, units)], own_sem.at[0])
    send_own(1, w_out)
    own_out.start()
    high, low = split_bf16(rows_t[...])
    rows_high[...] = high
    rows_low[...] = low

    for hop in range(1, parts):
        part_copy(hop).wait_recv()
    mine = pl.ds(me * units, units)
    total = d_part[:, my_block]
    for hop in range(1, parts):
        total = total + others[hop - 1]
    d_all[mine, my_block] = total * scale[:, my_block]
    send_own(0, d_all.at[mine, my_block])
    start_spread(me)

    early = max(steps - 1, 0)
    for step in range(early):
        pass_on(0, step)
    pass_on(1, 0)
    for step in range(early, steps):
        pass_on(0, step)

    for shard in range(size):
        for hop in range(1, parts):
            spread(hop, shard, lax.rem(part + parts - hop, parts)).wait_recv()

    width = 256

    @pl.loop(0, w_in.shape[1] // width)
    def _(tile):
        cols = pl.ds(pl.multiple_of(tile * width, width), width)
        d_high, d_low = split_bf16(d_all[cols, :])

        def product(left, right):
            return lax.dot_general(
                left, right, (((1,), (1,)), ((), ())), preferred_element_type=jnp.float32
            )

        grad = product(rows_high[...], d_high)
        grad = grad + (product(rows_low[...], d_high) + product(rows_high[...], d_low))
        weight, moment_one, moment_two, average = adamw(
            w_in[:, cols], m_in[:, cols], v_in[:, cols], e_in[:, cols], grad
        )
        w_new[:, cols] = weight
        m_new[:, cols] = moment_one
        v_new[:, cols] = moment_two
        e_new[:, cols] = average

    own_in = pltpu.make_async_copy(w_new, all_in.at[pl.ds(me * depth, depth)], own_sem.at[1])
    send_own(2, w_new)
    own_in.start()
    for step in range(steps):
        if step + 1 < steps:
            pass_on(1, step + 1)
        pass_on(2, step)
    for hop in range(1, parts):
        part_copy(hop).wait_send()
    for shard in range(size):
        for hop in range(1, parts):
            spread(hop, shard, part).wait_send()
    for kind in range(3):
        end_sends(kind)
    own_out.wait()
    own_in.wait()


def backward_tail(d_part, scale, rows_t, w_in, m_in, v_in, e_in, w_out):
    size, parts = lax.axis_size("tok"), lax.axis_size("inp")
    units, count = d_part.shape
    depth, wide = w_in.shape
    hops, steps = max(parts - 1, 1), max(size - 1, 1)
    in_vmem = pl.BlockSpec(memory_space=pltpu.VMEM)
    anywhere = pl.BlockSpec(memory_space=pl.ANY)
    shard = jax.ShapeDtypeStruct((depth, wide), jnp.float32)
    return pl.pallas_call(
        functools.partial(tail_kernel, size, parts),
        out_shape=(
            jax.ShapeDtypeStruct((size * depth, wide), jnp.float32),
            jax.ShapeDtypeStruct((size * units, w_out.shape[1]), jnp.float32),
            shard,
            shard,
            shard,
        ),
        in_specs=[in_vmem] * 7 + [anywhere],
        out_specs=(anywhere, anywhere, in_vmem, in_vmem, in_vmem),
        scratch_shapes=[
            pltpu.VMEM((hops, units, count // parts), jnp.float32),
            pltpu.VMEM((size * units, count), jnp.float32),
            pltpu.VMEM((depth, wide), jnp.float32),
            pltpu.VMEM((depth, count), jnp.bfloat16),
            pltpu.VMEM((depth, count), jnp.bfloat16),
            pltpu.SemaphoreType.DMA((hops,)),
            pltpu.SemaphoreType.DMA((hops,)),
            pltpu.SemaphoreType.DMA((3, 2, steps)),
            pltpu.SemaphoreType.DMA((3, 2, steps)),
            pltpu.SemaphoreType.DMA((hops, size)),
            pltpu.SemaphoreType.DMA((hops, size)),
            pltpu.SemaphoreType.DMA((2,)),
        ],
        compiler_params=pltpu.CompilerParams(
            collective_id=0, has_side_effects=True, vmem_limit_bytes=48 * 1024 * 1024
        ),
    )(d_part, scale, rows_t, w_in, m_in, v_in, e_in, w_out)


def sum_kernel(
    size,
    parts,
    given,
    result,
    from_inp,
    sums,
    from_tok,
    whole,
    inp_send,
    inp_recv,
    tok_send,
    tok_recv,
    back_send,
    back_recv,
):
    me = lax.axis_index("tok")
    part = lax.axis_index("inp")
    rows, block = sums.shape[1:]
    mesh_ids = pl.DeviceIdType.MESH

    def block_of(index):
        return pl.ds(pl.multiple_of(index * block, block), block)

    my_block = block_of(part)

    def inp_peer(hop):
        return lax.rem(part + hop, parts)

    def tok_at(turn):
        return lax.rem(me + 1 + turn, size)

    def rows_at(turn):
        return pl.ds(pl.multiple_of(tok_at(turn) * rows, rows), rows)

    barrier = pltpu.get_barrier_semaphore()
    for hop in range(1, parts):
        pl.semaphore_signal(
            barrier, inc=1, device_id={"inp": inp_peer(hop)}, device_id_type=mesh_ids
        )
    for turn in range(size - 1):
        pl.semaphore_signal(
            barrier, inc=1, device_id={"tok": tok_at(turn)}, device_id_type=mesh_ids
        )
    pl.semaphore_wait(barrier, parts - 1 + size - 1)

    def inp_copy(hop, turn):
        return pltpu.make_async_remote_copy(
            src_ref=given.at[rows_at(turn), block_of(inp_peer(hop))],
            dst_ref=from_inp.at[hop - 1, turn],
            send_sem=inp_send.at[hop - 1, turn],
            recv_sem=inp_recv.at[hop - 1, turn],
            device_id={"inp": inp_peer(hop)},
            device_id_type=mesh_ids,
        )

    def tok_copy(turn):
        return pltpu.make_async_remote_copy(
            src_ref=sums.at[turn],
            dst_ref=from_tok.at[turn],
            send_sem=tok_send.at[turn],
            recv_sem=tok_recv.at[turn],
            device_id={"tok": tok_at(turn)},
            device_id_type=mesh_ids,
        )

    def back_copy(hop, source):
        place = whole.at[:, block_of(source)]
        return pltpu.make_async_remote_copy(
            src_ref=place,
            dst_ref=place,
            send_sem=back_send.at[hop - 1],
            recv_sem=back_recv.at[hop - 1],
            device_id={"inp": inp_peer(hop)},
            device_id_type=mesh_ids,
        )

    for turn in range(size):
        for hop in range(1, parts):
            inp_copy(hop, turn).start()
    for turn in range(size):
        total = given[rows_at(turn), my_block]
        for hop in range(1, parts):
            inp_copy(hop, turn).wait_recv()
            total = total + from_inp[hop - 1, turn]
        sums[turn] = total
        if turn < size - 1:
            tok_copy(turn).start()
    total = sums[size - 1]
    for turn in range(size - 1):
        tok_copy(turn).wait_recv()
        total = total + from_tok[turn]
    whole[:, my_block] = total
    for hop in range(1, parts):
        back_copy(hop, part).start()
    for hop in range(1, parts):
        back_copy(hop, lax.rem(part + parts - hop, parts)).wait_recv()
    result[...] = whole[...]
    for hop in range(1, parts):
        back_copy(hop, part).wait_send()
        for turn in range(size):
            inp_copy(hop, turn).wait_send()
    for turn in range(size - 1):
        tok_copy(turn).wait_send()


def sum_hidden(given):
    size, parts = lax.axis_size("tok"), lax.axis_size("inp")
    rows, count = given.shape[0] // size, given.shape[1]
    hops, turns, block = max(parts - 1, 1), max(size - 1, 1), count // parts
    in_vmem = pl.BlockSpec(memory_space=pltpu.VMEM)
    return pl.pallas_call(
        functools.partial(sum_kernel, size, parts),
        out_shape=jax.ShapeDtypeStruct((rows, count), jnp.float32),
        in_specs=[in_vmem],
        out_specs=in_vmem,
        scratch_shapes=[
            pltpu.VMEM((hops, size, rows, block), jnp.float32),
            pltpu.VMEM((size, rows, block), jnp.float32),
            pltpu.VMEM((turns, rows, block), jnp.float32),
            pltpu.VMEM((rows, count), jnp.float32),
            pltpu.SemaphoreType.DMA((hops, size)),
            pltpu.SemaphoreType.DMA((hops, size)),
            pltpu.SemaphoreType.DMA((turns,)),
            pltpu.SemaphoreType.DMA((turns,)),
            pltpu.SemaphoreType.DMA((hops,)),
            pltpu.SemaphoreType.DMA((hops,)),
        ],
        compiler_params=pltpu.CompilerParams(
            collective_id=1, has_side_effects=True, vmem_limit_bytes=48 * 1024 * 1024
        ),
    )(given)


def on_device(
    tokens,
    targets,
    sample_ids,
    labels,
    utility,
    ref_loss,
    w_in,
    w_out,
    m_in,
    m_out,
    v_in,
    v_out,
    e_in,
    e_out,
):
    ids = gather_rows(gather_rows(sample_ids, "tok"), "hid")
    onehot = (ids[:, None] == jnp.arange(SAMPLES, dtype=jnp.int32)[None, :]).astype(jnp.float32)
    counts = jnp.sum(onehot, axis=0)
    columns = lax.all_to_all(tokens, "tok", split_axis=1, concat_axis=0, tiled=True)
    all_rows = gather_rows(columns, "hid")
    hidden_part = lax.dot_general(w_in, all_rows, (((0,), (1,)), ((), ())), precision=precise)
    hidden = sum_hidden(hidden_part)
    active, slope = gelu_parts(hidden)
    out_part = contract_rows(active, w_out)
    output = scatter_rows(scatter_rows(out_part, "hid"), "tok")
    output, onehot, counts = lax.optimization_barrier((output, onehot, counts))
    error = gather_rows(gather_rows(output - targets, "tok"), "hid")
    token_sq = jnp.sum(error * error, axis=1)
    sq_sums = lax.psum(jnp.dot(token_sq, onehot, precision=highest), "inp")
    loss, sample_coef = kto_terms(sq_sums, counts, labels, utility, ref_loss)
    token_coef = jnp.dot(onehot, sample_coef, precision=highest)
    grad_out = jnp.dot(active * token_coef[None, :], error, precision=precise)
    d_part = lax.dot_general(w_out, error, (((1,), (1,)), ((), ())), precision=precise)
    weight_out, new_m_out, new_v_out, new_e_out = adamw(w_out, m_out, v_out, e_out, grad_out)
    new_w_in, new_w_out, new_m_in, new_v_in, new_e_in = backward_tail(
        d_part, slope * token_coef[None, :], all_rows.T, w_in, m_in, v_in, e_in, weight_out
    )
    return (
        loss,
        new_w_in,
        new_w_out,
        new_m_in,
        new_m_out,
        new_v_in,
        new_v_out,
        new_e_in,
        new_e_out,
    )


def solution(mesh):
    in_specs = (
        P(("tok", "hid"), "inp"),
        P(("tok", "hid"), "inp"),
        P(("tok", "hid")),
        P(),
        P(),
        P(),
        P(("inp", "tok"), "hid"),
        P(("hid", "tok"), "inp"),
        P(("inp", "tok"), "hid"),
        P(("hid", "tok"), "inp"),
        P(("inp", "tok"), "hid"),
        P(("hid", "tok"), "inp"),
        P(("inp", "tok"), "hid"),
        P(("hid", "tok"), "inp"),
    )
    out_specs = (
        P(),
        P("inp", "hid"),
        P("hid", "inp"),
        P(("inp", "tok"), "hid"),
        P(("hid", "tok"), "inp"),
        P(("inp", "tok"), "hid"),
        P(("hid", "tok"), "inp"),
        P(("inp", "tok"), "hid"),
        P(("hid", "tok"), "inp"),
    )
    return jax.shard_map(
        on_device, mesh=mesh, in_specs=in_specs, out_specs=out_specs, check_vma=False
    )
```
